512 devices in a mesh: dp: 2 (over x_lo), ctx: 32 (over z, core), tp: 8 (over x_hi, y).
Axes of the slice: x: 4 (x_hi: 2, x_lo: 2; x = x_hi * 2 + x_lo), y: 4, z: 16, core: 2. Of those that a mesh axis runs over, the one named last changes fastest.
Arguments:
- query: bfloat16 [8192, 12288], P(('dp', 'ctx'), 'tp'), parts along dimension 0
- keys: bfloat16 [8192, 1024], P(('dp', 'ctx'), 'tp'), parts along dimension 0
- values: bfloat16 [8192, 1024], P(('dp', 'ctx'), 'tp'), parts along dimension 0, may hold values from -6 to 6
- doc_lengths: int32 [32], P('dp'), parts along dimension 0, may hold values from 1 to 2560, 4096 in all
- gain: bfloat16 [12288], P('tp'), may hold values from 0.5 to 1.5
Outputs:
- normed: bfloat16 [8192, 12288], P(('dp', 'ctx'), 'tp'), parts along dimension 0
The draws below stay inside these ranges and needn't reach their ends.
There are 2 independent parts, one for each index of `dp`. The reference program is written for one: setup_inputs(seed, part) draws one part's arguments, and reference() takes and returns one part's arrays. A program takes and returns all parts, laid end to end along the dimension named above; an argument that names none is the same for every part. Nothing has to cross between parts.
Inputs may be any that keep to these rules, and one draw needn't show every extreme that they name: `doc_lengths`: the lengths sum to 4096; the longest is exactly 2560.
All inputs are finite; a program needn't handle non-finite values.
Results may differ from the reference program's by a relative error of at most 0.015.
Values may be sent and summed in bfloat16 or wider, within the bound.
No kernel may reach another device: no remote copies, remote signals or barrier semaphores. Data moves between devices by JAX's collectives and lax.ppermute only.
A program may use at most 64 MiB of HBM per device.

```python
import math
import jax
import jax.numpy as jnp
import numpy as np
from jax import lax

QUERY_HEADS = 96
KEY_VALUE_HEADS = 8
HEAD_SIZE = 128
NDOC = 16
PACKED_TOKENS = 4096
LMAX = 2560


def paired_rows(key):
    key_query, random_key_pair = jax.random.split(key)
    queries = jnp.clip(jax.random.normal(key_query, (PACKED_TOKENS, QUERY_HEADS * HEAD_SIZE), jnp.float32), -6.0, 6.0)
    key_row_block = jnp.clip(jax.random.normal(random_key_pair, (PACKED_TOKENS, KEY_VALUE_HEADS * HEAD_SIZE), jnp.float32), -6.0, 6.0)
    return (queries, key_row_block)


def draw_query(key, part):
    return paired_rows(key)[0].astype(jnp.bfloat16)


def draw_keys(key, part):
    return paired_rows(key)[1].astype(jnp.bfloat16)


def levels(stream_key, dims, cuts, smallest, high):
    factor_of, own = 1.0, jax.random.fold_in(stream_key, 6)
    for axis_at, parts in cuts:
        draws = jnp.exp(jax.random.uniform(jax.random.fold_in(own, axis_at), (parts,), jnp.float32, smallest / len(cuts), high / len(cuts)))
        factor_of = factor_of * jnp.repeat(draws, dims[axis_at] // parts).reshape([-1 if axis == axis_at else 1 for axis in range(len(dims))])
    return factor_of


def length_profile(count, total, bound, slope):
    weights = [(1 << 20) // math.isqrt(grade ** slope) + 1 for grade in range(2, count + 1)]
    spare, given = total - bound - (count - 1), [1] * (count - 1)
    while spare > 0:
        candidates = [i for i in range(count - 1) if given[i] < bound]
        whole, remaining = sum([weights[i] for i in candidates]), spare
        for i in candidates:
            more = min(bound - given[i], max(1, remaining * weights[i] // whole), spare)
            given[i] = given[i] + more
            spare = spare - more
    return np.array([bound] + given)


def ragged_sizes(rng, amount, total, limit, skew):
    if amount == 2:
        one = jax.random.randint(rng, (), max(1, total - limit), min(limit, total - 1) + 1)
        return jnp.stack([one, total - one])
    lengths = jnp.asarray(length_profile(amount, total, limit, skew), jnp.int32)
    twos = (amount - 1) // 2
    donor, receiver = lengths[1:1 + 2 * twos:2], lengths[2:2 + 2 * twos:2]
    room = jnp.minimum(donor - 1, limit - receiver)
    passed = jax.random.randint(jax.random.fold_in(rng, 1), (twos,), 0, 1 << 20) % (room + 1)
    lengths = lengths.at[1:1 + 2 * twos:2].set(donor - passed).at[2:2 + 2 * twos:2].set(receiver + passed)
    return lengths[jax.random.permutation(jax.random.fold_in(rng, 2), amount)]


def gaussian(stream_key, shape, width, reach, cuts=(), held_as=jnp.bfloat16):
    drawn = width * jax.random.normal(stream_key, shape, jnp.float32)
    if cuts:
        drawn = drawn * levels(stream_key, shape, cuts, -0.22, 0.18)
    return jnp.clip(drawn, -reach, reach).astype(held_as)


def setup_inputs(seed: int = 0, part: int = 0) -> dict:
    key_of = jax.random.split(jax.random.key(seed), 6)
    part_splits = jax.random.split(jax.random.fold_in(key_of[5], part), 6)
    query = draw_query(jax.random.fold_in(jax.random.fold_in(key_of[5], part), 71), part)
    keys = draw_keys(jax.random.fold_in(jax.random.fold_in(key_of[5], part), 71), part)
    values = gaussian(part_splits[2], (PACKED_TOKENS, KEY_VALUE_HEADS * HEAD_SIZE), 1.0, 6.0, ((0, 32), (1, 8)))
    doc_lengths = ragged_sizes(part_splits[3], NDOC, PACKED_TOKENS, LMAX, 2).astype(jnp.int32)
    gain = jnp.clip(1.0 + 0.1 * jax.random.normal(key_of[4], (QUERY_HEADS * HEAD_SIZE,), jnp.float32), 0.5, 1.5).astype(jnp.bfloat16)
    return dict(query=query, keys=keys, values=values, doc_lengths=doc_lengths, gain=gain)


def reference(query, keys, values, doc_lengths, gain):
    ends = jnp.cumsum(doc_lengths).astype(jnp.int32)
    positions = jnp.arange(PACKED_TOKENS, dtype=jnp.int32)
    doc_of = lax.optimization_barrier(jnp.sum((positions[:, None] >= ends[None, :]).astype(jnp.int32), axis=1))
    allowed = (doc_of[:, None] == doc_of[None, :]) & (positions[None, :] <= positions[:, None])
    query_group_ratio = QUERY_HEADS // KEY_VALUE_HEADS
    scale = HEAD_SIZE ** (-0.5)

    def one_head(head):
        group = head // query_group_ratio
        q_rows = lax.dynamic_slice(query, (jnp.int32(0), (head * HEAD_SIZE).astype(jnp.int32)), (PACKED_TOKENS, HEAD_SIZE))
        k_rows = lax.dynamic_slice(keys, (jnp.int32(0), (group * HEAD_SIZE).astype(jnp.int32)), (PACKED_TOKENS, HEAD_SIZE))
        v_rows = lax.dynamic_slice(values, (jnp.int32(0), (group * HEAD_SIZE).astype(jnp.int32)), (PACKED_TOKENS, HEAD_SIZE))
        scores = jnp.dot(q_rows, k_rows.T, preferred_element_type=jnp.float32) * scale
        scores = jnp.where(allowed, scores, -1e+30)
        top = lax.optimization_barrier(jnp.max(scores, axis=1, keepdims=True))
        probs = jnp.where(allowed, jnp.exp(scores - top), 0.0)
        weights = (probs / lax.optimization_barrier(jnp.sum(probs, axis=1, keepdims=True))).astype(jnp.bfloat16)
        return jnp.dot(weights, v_rows, preferred_element_type=jnp.float32)
    heads = lax.map(one_head, jnp.arange(QUERY_HEADS, dtype=jnp.int32))
    context = jnp.transpose(heads, (1, 0, 2)).reshape(PACKED_TOKENS, QUERY_HEADS * HEAD_SIZE).astype(jnp.bfloat16)
    wide = context.astype(jnp.float32)
    power = lax.optimization_barrier(jnp.mean(wide * wide, axis=1, keepdims=True))
    return (wide * gain.astype(jnp.float32) / jnp.sqrt(power + 1e-06)).astype(jnp.bfloat16)
```

```python
import functools

import jax
import jax.numpy as jnp
from jax import lax
from jax.experimental import pallas as pl
from jax.experimental.pallas import tpu as pltpu
from jax.sharding import Mesh, PartitionSpec as P

QUERY_HEADS = 96
HEAD_SIZE = 128
ROWS = 128
MASKED = -1e30
EXP2_SCALE = HEAD_SIZE ** (-0.5) * 1.4426950408889634


def doc_starts(lengths_ref, q_pos):
    start = jnp.zeros_like(q_pos)
    end = jnp.int32(0)
    for i in range(lengths_ref.shape[0]):
        end = end + lengths_ref[i]
        start = jnp.maximum(start, jnp.where(q_pos >= end, end, 0))
    return start


def attend(step, distances, head_block, first, last, *refs):
    refs = list(refs)
    where_ref, lengths_ref, q_ref = refs[:3]
    pieces = refs[3 : 3 + len(distances)]
    rest = refs[3 + len(distances) :]
    if not first:
        m_in, l_in, acc_in = rest[:3]
        rest = rest[3:]
    if last:
        ctx_ref, squares_ref, bias_ref, k_ref, v_ref = rest
    else:
        m_out, l_out, acc_out, bias_ref, k_ref, v_ref = rest
    chip, core = where_ref[0], where_ref[1]
    q_pos = chip * (2 * ROWS) + core * ROWS + lax.broadcasted_iota(jnp.int32, (ROWS, ROWS), 0)
    start = doc_starts(lengths_ref, q_pos)
    lane = lax.broadcasted_iota(jnp.int32, (ROWS, ROWS), 1)
    at = 0
    for piece, (mine, back) in zip(pieces, distances):
        for j, d in enumerate(back):
            rows = pl.ds(at * ROWS, ROWS)
            k_ref[rows, :] = piece[j * ROWS : (j + 1) * ROWS, :HEAD_SIZE]
            v_ref[rows, :HEAD_SIZE] = piece[j * ROWS : (j + 1) * ROWS, HEAD_SIZE:]
            holder = core if mine else 1 - core
            k_pos = (chip - d) * (2 * ROWS) + holder * ROWS + lane
            allowed = (k_pos >= start) & (k_pos <= q_pos)
            bias_ref[:, rows] = jnp.where(allowed, 0.0, MASKED)
            at += 1
    v_ref[:, HEAD_SIZE:] = jnp.ones_like(v_ref[:, HEAD_SIZE:])
    squares = jnp.zeros((ROWS, HEAD_SIZE), jnp.float32)
    heads = q_ref.shape[1] // HEAD_SIZE
    for h0 in range(0, heads, head_block):
        q = jnp.concatenate(
            [q_ref[:, h * HEAD_SIZE : (h + 1) * HEAD_SIZE] for h in range(h0, h0 + head_block)], axis=0
        )
        s = lax.dot_general(q, k_ref[...], (((1,), (1,)), ((), ())), preferred_element_type=jnp.float32)
        s = s.reshape(head_block, ROWS, -1) + bias_ref[...][None]
        top = jnp.max(s, axis=-1, keepdims=True)
        if not first:
            m_old = m_in[h0 : h0 + head_block]
            top = jnp.maximum(top, m_old[:, :, :1])
        p = jnp.exp2((s - top) * EXP2_SCALE).astype(jnp.bfloat16)
        out = lax.dot_general(
            p.reshape(head_block * ROWS, -1), v_ref[...], (((1,), (0,)), ((), ())), preferred_element_type=jnp.float32
        ).reshape(head_block, ROWS, 2 * HEAD_SIZE)
        acc, total = out[:, :, :HEAD_SIZE], out[:, :, HEAD_SIZE:]
        if not first:
            correct = jnp.exp2((m_old - top) * EXP2_SCALE)
            acc = acc + acc_in[h0 : h0 + head_block] * correct
            total = total + l_in[h0 : h0 + head_block] * correct
        if last:
            context = (acc / total).astype(jnp.bfloat16)
            for h in range(head_block):
                ctx_ref[:, (h0 + h) * HEAD_SIZE : (h0 + h + 1) * HEAD_SIZE] = context[h]
                wide = context[h].astype(jnp.float32)
                squares = squares + wide * wide
        else:
            m_out[h0 : h0 + head_block] = jnp.broadcast_to(top, acc.shape)
            l_out[h0 : h0 + head_block] = total
            acc_out[h0 : h0 + head_block] = acc
    if last:
        summed = jnp.sum(squares.T, axis=0, keepdims=True)
        squares_ref[...] = jnp.broadcast_to(summed, squares_ref.shape)


def attention(where, lengths, query, pieces, distances, state, last, head_block):
    heads = query.shape[1] // HEAD_SIZE
    keys = sum(len(back) for _, back in distances) * ROWS
    vmem = pl.BlockSpec(memory_space=pltpu.VMEM)
    smem = pl.BlockSpec(memory_space=pltpu.SMEM)
    state = [] if state is None else list(state)
    if last:
        out_shape = (
            jax.ShapeDtypeStruct(query.shape, jnp.bfloat16),
            jax.ShapeDtypeStruct((8, ROWS), jnp.float32),
        )
    else:
        out_shape = (jax.ShapeDtypeStruct((heads, ROWS, HEAD_SIZE), jnp.float32),) * 3
    work = heads * ROWS * keys
    return pl.pallas_call(
        functools.partial(attend, 0, distances, head_block, not state, last),
        out_shape=out_shape,
        in_specs=[smem, smem] + [vmem] * (1 + len(pieces) + len(state)),
        out_specs=tuple([vmem] * len(out_shape)),
        scratch_shapes=[
            pltpu.VMEM((ROWS, keys), jnp.float32),
            pltpu.VMEM((keys, HEAD_SIZE), jnp.bfloat16),
            pltpu.VMEM((keys, 2 * HEAD_SIZE), jnp.bfloat16),
        ],
        compiler_params=pltpu.CompilerParams(vmem_limit_bytes=40 * 1024 * 1024),
        cost_estimate=pl.CostEstimate(flops=4 * work * HEAD_SIZE, bytes_accessed=4 << 20, transcendentals=work),
        name="attention_last" if last else "attention_first",
    )(where, lengths, query, *pieces, *state)


def scale_rows(ctx_ref, squares_ref, gain_ref, out_ref):
    power = jnp.sum(squares_ref[...], axis=0)[:1] / (QUERY_HEADS * HEAD_SIZE)
    factor = lax.rsqrt(jnp.broadcast_to(power, (ROWS, ROWS)).T + 1e-06)
    for h in range(ctx_ref.shape[1] // HEAD_SIZE):
        lanes = slice(h * HEAD_SIZE, (h + 1) * HEAD_SIZE)
        gain = gain_ref[:, lanes].astype(jnp.float32)
        out_ref[:, lanes] = (ctx_ref[:, lanes].astype(jnp.float32) * gain * factor).astype(jnp.bfloat16)


def body(query, keys, values, doc_lengths, gain):
    chips = lax.axis_size("chip")

    def shift(x, by):
        return lax.ppermute(x, "chip", [(i, (i + by) % chips) for i in range(chips)])

    def sibling(x):
        return lax.ppermute(x, "core", [(0, 1), (1, 0)])

    where = jnp.stack([lax.axis_index("chip"), lax.axis_index("core")]).astype(jnp.int32)
    own = jnp.concatenate([keys, values], axis=1)
    r1 = shift(own, 1)
    r2 = shift(own, 2)
    r10 = shift(own, -6)
    near = jnp.concatenate([own, r1, r2], axis=0)
    r9 = shift(r10, -1)
    r8 = shift(r10, -2)
    r7 = shift(r10, -3)
    r6 = shift(r2, 4)
    r345 = shift(near, 3)
    other_first = sibling(jnp.concatenate([near, r10], axis=0))
    state = attention(
        where, doc_lengths, query,
        (near, r10, other_first),
        ((True, (0, 1, 2)), (True, (10,)), (False, (0, 1, 2, 10))),
        None, False, 3,
    )
    other_last = sibling(jnp.concatenate([r345, r6, r7, r8, r9], axis=0))
    context, squares = attention(
        where, doc_lengths, query,
        (r345, r6, r7, r8, r9, other_last),
        ((True, (3, 4, 5)), (True, (6,)), (True, (7,)), (True, (8,)), (True, (9,)), (False, (3, 4, 5, 6, 7, 8, 9))),
        state, True, 2,
    )
    all_squares = lax.all_to_all(jnp.broadcast_to(squares, (8,) + squares.shape), "tp", 0, 0)
    return pl.pallas_call(
        scale_rows,
        out_shape=jax.ShapeDtypeStruct(query.shape, jnp.bfloat16),
        compiler_params=pltpu.CompilerParams(vmem_limit_bytes=16 * 1024 * 1024),
    )(context, all_squares, gain.reshape(1, -1))


def solution(mesh):
    sizes = mesh.shape
    fine = Mesh(
        mesh.devices.reshape(sizes["dp"], sizes["ctx"] // 2, 2, sizes["tp"]), ("dp", "chip", "core", "tp")
    )
    tokens = ("dp", "chip", "core")
    return jax.shard_map(
        body,
        mesh=fine,
        in_specs=(P(tokens, "tp"), P(tokens, "tp"), P(tokens, "tp"), P("dp"), P("tp")),
        out_specs=P(tokens, "tp"),
        check_vma=False,
    )
```

```python
import functools

import jax
import jax.numpy as jnp
from jax import lax
from jax.experimental import pallas as pl
from jax.experimental.pallas import tpu as pltpu
from jax.sharding import Mesh, PartitionSpec as P

QUERY_HEADS = 96
HEAD_SIZE = 128
ROWS = 128
MASKED = -1e30
EXP2_SCALE = HEAD_SIZE ** (-0.5) * 1.4426950408889634


def doc_starts(lengths_ref, q_pos):
    start = jnp.zeros_like(q_pos)
    end = jnp.int32(0)
    for i in range(lengths_ref.shape[0]):
        end = end + lengths_ref[i]
        start = jnp.maximum(start, jnp.where(q_pos >= end, end, 0))
    return start


def attend(layout, head_block, first, last, *refs):
    refs = list(refs)
    where_ref, lengths_ref, q_ref = refs[:3]
    pieces = refs[3 : 3 + len(layout)]
    rest = refs[3 + len(layout) :]
    if not first:
        m_in, l_in, acc_in = rest[:3]
        rest = rest[3:]
    if last:
        gain_ref, product_ref, squares_ref, bias_ref, k_ref, v_ref = rest
    else:
        m_out, l_out, acc_out, bias_ref, k_ref, v_ref = rest
    chip, core = where_ref[0], where_ref[1]
    q_pos = chip * (2 * ROWS) + core * ROWS + lax.broadcasted_iota(jnp.int32, (ROWS, ROWS), 0)
    start = doc_starts(lengths_ref, q_pos)
    lane = lax.broadcasted_iota(jnp.int32, (ROWS, ROWS), 1)
    at = 0
    for piece, blocks in zip(pieces, layout):
        for j, block in enumerate(blocks):
            if block is None:
                continue
            back, half = block
            rows = pl.ds(at * ROWS, ROWS)
            k_ref[rows, :] = piece[j * ROWS : (j + 1) * ROWS, :HEAD_SIZE]
            v_ref[rows, :HEAD_SIZE] = piece[j * ROWS : (j + 1) * ROWS, HEAD_SIZE:]
            k_pos = (chip - back) * (2 * ROWS) + half * ROWS + lane
            allowed = (k_pos >= start) & (k_pos <= q_pos)
            bias_ref[:, rows] = jnp.where(allowed, 0.0, MASKED)
            at += 1
    v_ref[:, HEAD_SIZE:] = jnp.ones_like(v_ref[:, HEAD_SIZE:])
    squares = jnp.zeros((ROWS, HEAD_SIZE), jnp.float32)
    heads = q_ref.shape[1] // HEAD_SIZE
    for h0 in range(0, heads, head_block):
        q = jnp.concatenate(
            [q_ref[:, h * HEAD_SIZE : (h + 1) * HEAD_SIZE] for h in range(h0, h0 + head_block)], axis=0
        )
        s = lax.dot_general(q, k_ref[...], (((1,), (1,)), ((), ())), preferred_element_type=jnp.float32)
        s = s.reshape(head_block, ROWS, -1) + bias_ref[...][None]
        top = jnp.max(s, axis=-1, keepdims=True)
        if not first:
            m_old = m_in[h0 : h0 + head_block]
            top = jnp.maximum(top, m_old[:, :, :1])
        p = jnp.exp2((s - top) * EXP2_SCALE).astype(jnp.bfloat16)
        out = lax.dot_general(
            p.reshape(head_block * ROWS, -1), v_ref[...], (((1,), (0,)), ((), ())), preferred_element_type=jnp.float32
        ).reshape(head_block, ROWS, 2 * HEAD_SIZE)
        acc, total = out[:, :, :HEAD_SIZE], out[:, :, HEAD_SIZE:]
        if not first:
            correct = jnp.exp2((m_old - top) * EXP2_SCALE)
            acc = acc + acc_in[h0 : h0 + head_block] * correct
            total = total + l_in[h0 : h0 + head_block] * correct
        if last:
            context = (acc / total).astype(jnp.bfloat16)
            for h in range(head_block):
                lanes = slice((h0 + h) * HEAD_SIZE, (h0 + h + 1) * HEAD_SIZE)
                wide = context[h].astype(jnp.float32)
                product_ref[:, lanes] = wide * gain_ref[:, lanes].astype(jnp.float32)
                squares = squares + wide * wide
        else:
            m_out[h0 : h0 + head_block] = jnp.broadcast_to(top, acc.shape)
            l_out[h0 : h0 + head_block] = total
            acc_out[h0 : h0 + head_block] = acc
    if last:
        summed = jnp.sum(squares.T, axis=0, keepdims=True)
        squares_ref[...] = jnp.broadcast_to(summed[None], squares_ref.shape)


def attention(where, lengths, query, pieces, layout, state, gain, head_block):
    heads = query.shape[1] // HEAD_SIZE
    keys = sum(block is not None for blocks in layout for block in blocks) * ROWS
    last = gain is not None
    vmem = pl.BlockSpec(memory_space=pltpu.VMEM)
    smem = pl.BlockSpec(memory_space=pltpu.SMEM)
    state = [] if state is None else list(state)
    tail = [gain] if last else []
    if last:
        out_shape = (
            jax.ShapeDtypeStruct(query.shape, jnp.float32),
            jax.ShapeDtypeStruct((lax.axis_size("tp"), 8, ROWS), jnp.float32),
        )
    else:
        out_shape = (jax.ShapeDtypeStruct((heads, ROWS, HEAD_SIZE), jnp.float32),) * 3
    work = heads * ROWS * keys
    return pl.pallas_call(
        functools.partial(attend, layout, head_block, not state, last),
        out_shape=out_shape,
        in_specs=[smem, smem] + [vmem] * (1 + len(pieces) + len(state) + len(tail)),
        out_specs=tuple([vmem] * len(out_shape)),
        scratch_shapes=[
            pltpu.VMEM((ROWS, keys), jnp.float32),
            pltpu.VMEM((keys, HEAD_SIZE), jnp.bfloat16),
            pltpu.VMEM((keys, 2 * HEAD_SIZE), jnp.bfloat16),
        ],
        compiler_params=pltpu.CompilerParams(vmem_limit_bytes=40 * 1024 * 1024),
        cost_estimate=pl.CostEstimate(flops=4 * work * HEAD_SIZE, bytes_accessed=4 << 20, transcendentals=work),
        name="attention_last" if last else "attention_first",
    )(where, lengths, query, *pieces, *state, *tail)


def scale_rows(product_ref, squares_ref, out_ref):
    power = jnp.sum(squares_ref[...], axis=0)[:1] / (QUERY_HEADS * HEAD_SIZE)
    factor = lax.rsqrt(jnp.broadcast_to(power, (ROWS, ROWS)).T + 1e-06)
    for h in range(product_ref.shape[1] // HEAD_SIZE):
        lanes = slice(h * HEAD_SIZE, (h + 1) * HEAD_SIZE)
        out_ref[:, lanes] = (product_ref[:, lanes] * factor).astype(jnp.bfloat16)


def halves(*distances):
    return [(back, half) for back in distances for half in (0, 1)]


def body(query, keys, values, doc_lengths, gain):
    chips = lax.axis_size("chip")
    core = lax.axis_index("core")

    def send(x, by):
        pairs = []
        for k in (0, 1):
            if by[k] is not None:
                pairs += [(z * 2 + k, (z + by[k]) % chips * 2 + k) for z in range(chips)]
        return lax.ppermute(x, ("chip", "core"), pairs)

    def share(x):
        return lax.all_gather(x, "core", axis=0, tiled=True)

    where = jnp.stack([lax.axis_index("chip"), core]).astype(jnp.int32)
    own = share(jnp.concatenate([keys, values], axis=1))
    r1_10 = send(own, (1, -6))
    r2 = send(own, (2, None))
    r345 = send(jnp.concatenate([own, r1_10, r2], axis=0), (3, None))
    r9 = send(r1_10, (None, -1))
    r87 = send(jnp.concatenate([r1_10, r9], axis=0), (None, -2))
    up = core == 0
    r6 = send(jnp.where(up, r2[:ROWS], r1_10[ROWS:]), (4, -4))
    b1_10, b2, b9 = lax.optimization_barrier((r1_10, r2, r9))
    first = share(jnp.concatenate([b1_10, jnp.where(up, b2, b9)], axis=0))
    state = attention(
        where, doc_lengths, query, (own, first),
        (halves(0), halves(1, 2, 10, 9)),
        None, None, 2,
    )
    second = share(
        jnp.where(up, jnp.concatenate([r345, r6], axis=0), jnp.concatenate([r87, r6, r345[: 2 * ROWS]], axis=0))
    )
    product, squares = attention(
        where, doc_lengths, query, (second,),
        (halves(3, 4, 5) + [(6, 0)] + halves(8, 7) + [(6, 1)] + [None] * 2,),
        state, gain.reshape(1, -1), 1,
    )
    all_squares = lax.all_to_all(squares, "tp", 0, 0)
    return pl.pallas_call(
        scale_rows,
        out_shape=jax.ShapeDtypeStruct(query.shape, jnp.bfloat16),
        compiler_params=pltpu.CompilerParams(vmem_limit_bytes=16 * 1024 * 1024),
    )(product, all_squares)


def solution(mesh):
    sizes = mesh.shape
    fine = Mesh(
        mesh.devices.reshape(sizes["dp"], sizes["ctx"] // 2, 2, sizes["tp"]), ("dp", "chip", "core", "tp")
    )
    tokens = ("dp", "chip", "core")
    return jax.shard_map(
        body,
        mesh=fine,
        in_specs=(P(tokens, "tp"), P(tokens, "tp"), P(tokens, "tp"), P("dp"), P("tp")),
        out_specs=P(tokens, "tp"),
        check_vma=False,
    )
```

```python
import functools

import jax
import jax.numpy as jnp
from jax import lax
from jax.experimental import pallas as pl
from jax.experimental.pallas import tpu as pltpu
from jax.sharding import Mesh, PartitionSpec as P

QUERY_HEADS = 96
HEAD_SIZE = 128
ROWS = 128
MASKED = -1e30
EXP2_SCALE = HEAD_SIZE ** (-0.5) * 1.4426950408889634


def doc_starts(lengths_ref, q_pos):
    start = jnp.zeros_like(q_pos)
    end = jnp.int32(0)
    for i in range(lengths_ref.shape[0]):
        end = end + lengths_ref[i]
        start = jnp.maximum(start, jnp.where(q_pos >= end, end, 0))
    return start


def attend(layout, head_block, first, last, *refs):
    refs = list(refs)
    where_ref, lengths_ref, q_ref = refs[:3]
    pieces = refs[3 : 3 + len(layout)]
    rest = refs[3 + len(layout) :]
    if not first:
        m_in, l_in, acc_in = rest[:3]
        rest = rest[3:]
    if last:
        gain_ref, product_ref, squares_ref, bias_ref, k_ref, v_ref = rest
    else:
        m_out, l_out, acc_out, bias_ref, k_ref, v_ref = rest
    chip, core = where_ref[0], where_ref[1]
    q_pos = chip * (2 * ROWS) + core * ROWS + lax.broadcasted_iota(jnp.int32, (ROWS, ROWS), 0)
    start = doc_starts(lengths_ref, q_pos)
    lane = lax.broadcasted_iota(jnp.int32, (ROWS, ROWS), 1)
    at = 0
    for piece, blocks in zip(pieces, layout):
        for j, block in enumerate(blocks):
            if block is None:
                continue
            back, half = block
            rows = pl.ds(at * ROWS, ROWS)
            k_ref[rows, :] = piece[j * ROWS : (j + 1) * ROWS, :HEAD_SIZE]
            v_ref[rows, :HEAD_SIZE] = piece[j * ROWS : (j + 1) * ROWS, HEAD_SIZE:]
            k_pos = (chip - back) * (2 * ROWS) + half * ROWS + lane
            allowed = (k_pos >= start) & (k_pos <= q_pos)
            bias_ref[:, rows] = jnp.where(allowed, 0.0, MASKED)
            at += 1
    v_ref[:, HEAD_SIZE:] = jnp.ones_like(v_ref[:, HEAD_SIZE:])
    squares = jnp.zeros((ROWS, HEAD_SIZE), jnp.float32)
    heads = q_ref.shape[1] // HEAD_SIZE
    for h0 in range(0, heads, head_block):
        q = jnp.concatenate(
            [q_ref[:, h * HEAD_SIZE : (h + 1) * HEAD_SIZE] for h in range(h0, h0 + head_block)], axis=0
        )
        s = lax.dot_general(q, k_ref[...], (((1,), (1,)), ((), ())), preferred_element_type=jnp.float32)
        s = s.reshape(head_block, ROWS, -1) + bias_ref[...][None]
        top = jnp.max(s, axis=-1, keepdims=True)
        if not first:
            m_old = m_in[h0 : h0 + head_block]
            top = jnp.maximum(top, m_old[:, :, :1])
        p = jnp.exp2((s - top) * EXP2_SCALE).astype(jnp.bfloat16)
        out = lax.dot_general(
            p.reshape(head_block * ROWS, -1), v_ref[...], (((1,), (0,)), ((), ())), preferred_element_type=jnp.float32
        ).reshape(head_block, ROWS, 2 * HEAD_SIZE)
        acc, total = out[:, :, :HEAD_SIZE], out[:, :, HEAD_SIZE:]
        if not first:
            correct = jnp.exp2((m_old - top) * EXP2_SCALE)
            acc = acc + acc_in[h0 : h0 + head_block] * correct
            total = total + l_in[h0 : h0 + head_block] * correct
        if last:
            context = (acc / total).astype(jnp.bfloat16)
            for h in range(head_block):
                lanes = slice((h0 + h) * HEAD_SIZE, (h0 + h + 1) * HEAD_SIZE)
                wide = context[h].astype(jnp.float32)
                product_ref[:, lanes] = wide * gain_ref[:, lanes].astype(jnp.float32)
                squares = squares + wide * wide
        else:
            m_out[h0 : h0 + head_block] = jnp.broadcast_to(top, acc.shape)
            l_out[h0 : h0 + head_block] = total
            acc_out[h0 : h0 + head_block] = acc
    if last:
        summed = jnp.sum(squares.T, axis=0, keepdims=True)
        squares_ref[...] = jnp.broadcast_to(summed[None], squares_ref.shape)


def attention(where, lengths, query, pieces, layout, state, gain, head_block):
    heads = query.shape[1] // HEAD_SIZE
    keys = sum(block is not None for blocks in layout for block in blocks) * ROWS
    last = gain is not None
    vmem = pl.BlockSpec(memory_space=pltpu.VMEM)
    smem = pl.BlockSpec(memory_space=pltpu.SMEM)
    state = [] if state is None else list(state)
    tail = [gain] if last else []
    if last:
        out_shape = (
            jax.ShapeDtypeStruct(query.shape, jnp.float32),
            jax.ShapeDtypeStruct((lax.axis_size("tp"), 8, ROWS), jnp.float32),
        )
    else:
        out_shape = (jax.ShapeDtypeStruct((heads, ROWS, HEAD_SIZE), jnp.float32),) * 3
    work = heads * ROWS * keys
    return pl.pallas_call(
        functools.partial(attend, layout, head_block, not state, last),
        out_shape=out_shape,
        in_specs=[smem, smem] + [vmem] * (1 + len(pieces) + len(state) + len(tail)),
        out_specs=tuple([vmem] * len(out_shape)),
        scratch_shapes=[
            pltpu.VMEM((ROWS, keys), jnp.float32),
            pltpu.VMEM((keys, HEAD_SIZE), jnp.bfloat16),
            pltpu.VMEM((keys, 2 * HEAD_SIZE), jnp.bfloat16),
        ],
        compiler_params=pltpu.CompilerParams(vmem_limit_bytes=40 * 1024 * 1024),
        cost_estimate=pl.CostEstimate(flops=4 * work * HEAD_SIZE, bytes_accessed=4 << 20, transcendentals=work),
        name="attention_last" if last else "attention_first",
    )(where, lengths, query, *pieces, *state, *tail)


def scale_rows(product_ref, squares_ref, out_ref):
    power = jnp.sum(squares_ref[...], axis=0)[:1] / (QUERY_HEADS * HEAD_SIZE)
    factor = lax.rsqrt(jnp.broadcast_to(power, (ROWS, ROWS)).T + 1e-06)
    for h in range(product_ref.shape[1] // HEAD_SIZE):
        lanes = slice(h * HEAD_SIZE, (h + 1) * HEAD_SIZE)
        out_ref[:, lanes] = (product_ref[:, lanes] * factor).astype(jnp.bfloat16)


def halves(*distances):
    return [(back, half) for back in distances for half in (0, 1)]


def body(query, keys, values, doc_lengths, gain):
    chips = lax.axis_size("chip")
    core = lax.axis_index("core")

    def send(x, up=(), down=()):
        pairs = []
        for k, way in enumerate((up, down)):
            if way:
                by, senders = way
                pairs += [(z * 2 + k, (z + by) % chips * 2 + k) for z in senders]
        return lax.ppermute(x, ("chip", "core"), pairs)

    def share(x):
        return lax.all_gather(x, "core", axis=0, tiled=True)

    where = jnp.stack([lax.axis_index("chip"), core]).astype(jnp.int32)
    own = share(jnp.concatenate([keys, values], axis=1))
    r1_10 = send(own, up=(1, range(chips - 1)), down=(-6, range(chips - 6)))
    r2 = send(own, up=(2, range(chips - 2)))
    r6 = send(own, down=(6, range(chips - 6)))
    r345 = send(jnp.concatenate([own, r1_10, r2], axis=0), up=(3, range(chips - 3)))
    r9 = send(r1_10, down=(-1, [0, 1, 2, *range(10, chips)]))
    r87 = send(jnp.concatenate([r1_10, r9], axis=0), down=(-2, [0, 1, *range(9, chips)]))
    up = core == 0
    b1_10, b2, b9, b6 = lax.optimization_barrier((r1_10, r2, r9, r6))
    first = share(jnp.concatenate([b1_10, jnp.where(up, b2, b9), b6], axis=0))
    state = attention(
        where, doc_lengths, query, (own, first),
        (halves(0), halves(1, 2) + [None, None] + halves(10, 9, 6)),
        None, None, 2,
    )
    second = share(jnp.where(up, r345, jnp.concatenate([r87, r345[: 2 * ROWS]], axis=0)))
    product, squares = attention(
        where, doc_lengths, query, (second,),
        (halves(3, 4, 5, 8, 7) + [None, None],),
        state, gain.reshape(1, -1), 1,
    )
    all_squares = lax.all_to_all(squares, "tp", 0, 0)
    return pl.pallas_call(
        scale_rows,
        out_shape=jax.ShapeDtypeStruct(query.shape, jnp.bfloat16),
        compiler_params=pltpu.CompilerParams(vmem_limit_bytes=16 * 1024 * 1024),
    )(product, all_squares)


def solution(mesh):
    sizes = mesh.shape
    fine = Mesh(
        mesh.devices.reshape(sizes["dp"], sizes["ctx"] // 2, 2, sizes["tp"]), ("dp", "chip", "core", "tp")
    )
    tokens = ("dp", "chip", "core")
    return jax.shard_map(
        body,
        mesh=fine,
        in_specs=(P(tokens, "tp"), P(tokens, "tp"), P(tokens, "tp"), P("dp"), P("tp")),
        out_specs=P(tokens, "tp"),
        check_vma=False,
    )
```

```python
import functools

import jax
import jax.numpy as jnp
from jax import lax
from jax.experimental import pallas as pl
from jax.experimental.pallas import tpu as pltpu
from jax.sharding import Mesh, PartitionSpec as P

QUERY_HEADS = 96
HEAD_SIZE = 128
ROWS = 128
MASKED = -1e30
EXP2_SCALE = HEAD_SIZE ** (-0.5) * 1.4426950408889634


def doc_starts(lengths_ref, q_pos):
    start = jnp.zeros_like(q_pos)
    end = jnp.int32(0)
    for i in range(lengths_ref.shape[0]):
        end = end + lengths_ref[i]
        start = jnp.maximum(start, jnp.where(q_pos >= end, end, 0))
    return start


def attend(layout, head_block, first, last, *refs):
    refs = list(refs)
    where_ref, lengths_ref, q_ref = refs[:3]
    pieces = refs[3 : 3 + len(layout)]
    rest = refs[3 + len(layout) :]
    if not first:
        m_in, l_in, acc_in = rest[:3]
        rest = rest[3:]
    if last:
        gain_ref, product_ref, squares_ref, bias_ref, k_ref, v_ref = rest
    else:
        m_out, l_out, acc_out, bias_ref, k_ref, v_ref = rest
    chip, core = where_ref[0], where_ref[1]
    q_pos = chip * (2 * ROWS) + core * ROWS + lax.broadcasted_iota(jnp.int32, (ROWS, ROWS), 0)
    start = doc_starts(lengths_ref, q_pos)
    lane = lax.broadcasted_iota(jnp.int32, (ROWS, ROWS), 1)
    at = 0
    for piece, blocks in zip(pieces, layout):
        for j, block in enumerate(blocks):
            if block is None:
                continue
            back, half = block
            rows = pl.ds(at * ROWS, ROWS)
            k_ref[rows, :] = piece[j * ROWS : (j + 1) * ROWS, :HEAD_SIZE]
            v_ref[rows, :HEAD_SIZE] = piece[j * ROWS : (j + 1) * ROWS, HEAD_SIZE:]
            k_pos = (chip - back) * (2 * ROWS) + half * ROWS + lane
            allowed = (k_pos >= start) & (k_pos <= q_pos)
            bias_ref[:, rows] = jnp.where(allowed, 0.0, MASKED)
            at += 1
    v_ref[:, HEAD_SIZE:] = jnp.ones_like(v_ref[:, HEAD_SIZE:])
    squares = jnp.zeros((ROWS, HEAD_SIZE), jnp.float32)
    heads = q_ref.shape[1] // HEAD_SIZE
    for h0 in range(0, heads, head_block):
        q = jnp.concatenate(
            [q_ref[:, h * HEAD_SIZE : (h + 1) * HEAD_SIZE] for h in range(h0, h0 + head_block)], axis=0
        )
        s = lax.dot_general(q, k_ref[...], (((1,), (1,)), ((), ())), preferred_element_type=jnp.float32)
        s = s.reshape(head_block, ROWS, -1) + bias_ref[...][None]
        top = jnp.max(s, axis=-1, keepdims=True)
        if not first:
            m_old = m_in[h0 : h0 + head_block]
            top = jnp.maximum(top, m_old[:, :, :1])
        p = jnp.exp2((s - top) * EXP2_SCALE).astype(jnp.bfloat16)
        out = lax.dot_general(
            p.reshape(head_block * ROWS, -1), v_ref[...], (((1,), (0,)), ((), ())), preferred_element_type=jnp.float32
        ).reshape(head_block, ROWS, 2 * HEAD_SIZE)
        acc, total = out[:, :, :HEAD_SIZE], out[:, :, HEAD_SIZE:]
        if not first:
            correct = jnp.exp2((m_old - top) * EXP2_SCALE)
            acc = acc + acc_in[h0 : h0 + head_block] * correct
            total = total + l_in[h0 : h0 + head_block] * correct
        if last:
            context = (acc / total).astype(jnp.bfloat16)
            for h in range(head_block):
                lanes = slice((h0 + h) * HEAD_SIZE, (h0 + h + 1) * HEAD_SIZE)
                wide = context[h].astype(jnp.float32)
                product_ref[:, lanes] = wide * gain_ref[:, lanes].astype(jnp.float32)
                squares = squares + wide * wide
        else:
            m_out[h0 : h0 + head_block] = jnp.broadcast_to(top, acc.shape)
            l_out[h0 : h0 + head_block] = total
            acc_out[h0 : h0 + head_block] = acc
    if last:
        summed = jnp.sum(squares.T, axis=0, keepdims=True)
        squares_ref[...] = jnp.broadcast_to(summed[None], squares_ref.shape)


def attention(where, lengths, query, pieces, layout, state, gain, head_block):
    heads = query.shape[1] // HEAD_SIZE
    keys = sum(block is not None for blocks in layout for block in blocks) * ROWS
    last = gain is not None
    vmem = pl.BlockSpec(memory_space=pltpu.VMEM)
    smem = pl.BlockSpec(memory_space=pltpu.SMEM)
    state = [] if state is None else list(state)
    tail = [gain] if last else []
    if last:
        out_shape = (
            jax.ShapeDtypeStruct(query.shape, jnp.float32),
            jax.ShapeDtypeStruct((lax.axis_size("tp"), 8, ROWS), jnp.float32),
        )
    else:
        out_shape = (jax.ShapeDtypeStruct((heads, ROWS, HEAD_SIZE), jnp.float32),) * 3
    work = heads * ROWS * keys
    return pl.pallas_call(
        functools.partial(attend, layout, head_block, not state, last),
        out_shape=out_shape,
        in_specs=[smem, smem] + [vmem] * (1 + len(pieces) + len(state) + len(tail)),
        out_specs=tuple([vmem] * len(out_shape)),
        scratch_shapes=[
            pltpu.VMEM((ROWS, keys), jnp.float32),
            pltpu.VMEM((keys, HEAD_SIZE), jnp.bfloat16),
            pltpu.VMEM((keys, 2 * HEAD_SIZE), jnp.bfloat16),
        ],
        compiler_params=pltpu.CompilerParams(vmem_limit_bytes=40 * 1024 * 1024),
        cost_estimate=pl.CostEstimate(flops=4 * work * HEAD_SIZE, bytes_accessed=4 << 20, transcendentals=work),
        name="attention_last" if last else "attention_first",
    )(where, lengths, query, *pieces, *state, *tail)


def scale_rows(product_ref, squares_ref, out_ref):
    power = jnp.sum(squares_ref[...], axis=0)[:1] / (QUERY_HEADS * HEAD_SIZE)
    factor = lax.rsqrt(jnp.broadcast_to(power, (ROWS, ROWS)).T + 1e-06)
    for h in range(product_ref.shape[1] // HEAD_SIZE):
        lanes = slice(h * HEAD_SIZE, (h + 1) * HEAD_SIZE)
        out_ref[:, lanes] = (product_ref[:, lanes] * factor).astype(jnp.bfloat16)


def halves(*distances):
    return [(back, half) for back in distances for half in (0, 1)]


def body(query, keys, values, doc_lengths, gain):
    chips = lax.axis_size("chip")
    core = lax.axis_index("core")

    def send(x, up=(), down=()):
        pairs = []
        for k, way in enumerate((up, down)):
            if way:
                by, senders = way
                pairs += [(z * 2 + k, (z + by) % chips * 2 + k) for z in senders]
        return lax.ppermute(x, ("chip", "core"), pairs)

    def share(x):
        return lax.all_gather(x, "core", axis=0, tiled=True)

    where = jnp.stack([lax.axis_index("chip"), core]).astype(jnp.int32)
    own = share(jnp.concatenate([keys, values], axis=1))
    r1_10 = send(own, up=(1, range(chips - 1)), down=(-6, range(chips - 6)))
    r2 = send(own, up=(2, range(chips - 2)))
    late, _ = lax.optimization_barrier((own, r1_10))
    r6 = send(late, down=(6, range(chips - 6)))
    r345 = send(jnp.concatenate([own, r1_10, r2], axis=0), up=(3, range(chips - 3)))
    r9 = send(r1_10, down=(-1, [0, 1, 2, *range(10, chips)]))
    r87 = send(jnp.concatenate([r1_10, r9], axis=0), down=(-2, [0, 1, *range(9, chips)]))
    up = core == 0
    b1_10, b2, b9 = lax.optimization_barrier((r1_10, r2, r9))
    first = share(jnp.concatenate([b1_10, jnp.where(up, b2, b9)], axis=0))
    state = attention(
        where, doc_lengths, query, (own, first),
        (halves(0), halves(1, 2, 10, 9)),
        None, None, 2,
    )
    second = share(jnp.where(up, r345, jnp.concatenate([r87, r6], axis=0)))
    product, squares = attention(
        where, doc_lengths, query, (second,),
        (halves(3, 4, 5, 8, 7, 6),),
        state, gain.reshape(1, -1), 1,
    )
    all_squares = lax.all_to_all(squares, "tp", 0, 0)
    return pl.pallas_call(
        scale_rows,
        out_shape=jax.ShapeDtypeStruct(query.shape, jnp.bfloat16),
        compiler_params=pltpu.CompilerParams(vmem_limit_bytes=16 * 1024 * 1024),
    )(product, all_squares)


def solution(mesh):
    sizes = mesh.shape
    fine = Mesh(
        mesh.devices.reshape(sizes["dp"], sizes["ctx"] // 2, 2, sizes["tp"]), ("dp", "chip", "core", "tp")
    )
    tokens = ("dp", "chip", "core")
    return jax.shard_map(
        body,
        mesh=fine,
        in_specs=(P(tokens, "tp"), P(tokens, "tp"), P(tokens, "tp"), P("dp"), P("tp")),
        out_specs=P(tokens, "tp"),
        check_vma=False,
    )
```
